256 devices in a mesh: span: 4 (over z_hi, core), head: 16 (over z_lo, x), rep: 4 (over y).
Axes of the slice: x: 4, y: 4, z: 8 (z_hi: 2, z_lo: 4; z = z_hi * 4 + z_lo), core: 2. Of those that a mesh axis runs over, the one named last changes fastest.
Arguments:
- queries: bfloat16 [16384, 6144], P(('rep', 'span', 'head')), parts along dimension 0, may hold values from -10 to 10
- key_value: bfloat16 [16384, 2, 1024], P(('rep', 'span', 'head')), parts along dimension 0, may hold values from -4 to 4
- w_out: bfloat16 [6144, 6144], P('head'), may hold values from -0.078125 to 0.078125
- gate_table: bfloat16 [64, 6144], replicated, may hold values from 0.25 to 2
- levels: int32 [16], P('rep'), parts along dimension 0, may hold values from 0 to 63
- span_mask: int32 [16, 4], P('rep'), parts along dimension 0, may hold values from 0 to 1, as said below
- counts: int32 [16], P('rep'), parts along dimension 0, may hold values from 512 to 1024, as said below
Outputs:
- output: bfloat16 [16384, 6144], P(('rep', 'span', 'head')), parts along dimension 0
The draws below stay inside these ranges and needn't reach their ends.
There are 4 independent parts, one for each index of `rep`. The reference program is written for one: setup_inputs(seed, part) draws one part's arguments, and reference() takes and returns one part's arrays. A program takes and returns all parts, laid end to end along the dimension named above; an argument that names none is the same for every part. Nothing has to cross between parts.
Inputs may be any that keep to these rules, and one draw needn't show every extreme that they name: span_mask[i, i] = 1 and span_mask[i, i - 1] = 1; span_mask[i, j] = 0 for j > i; the entries for j < i - 1 are drawn. `counts`: in every video one span has exactly 1024 live tokens and another exactly 512.
All inputs are finite; a program needn't handle non-finite values.
Results may differ from the reference program's by a relative error of at most 0.024.
Values may be sent and summed in bfloat16 or wider, within the bound.
A program may use at most 64 MiB of HBM per device.

```python
import jax
import jax.numpy as jnp
from jax import lax

D = 6144
HEADS = 48
HD = 128
KV_GROUPS = 8
LEVELS = 64
SPAN_TOKENS = 1024
SPANS = 4
TOKENS = 4096
KV_COLS = 1024
N_HEAD = 16


def draw_queries(key, part):
    key = jax.random.fold_in(key, 11)
    noise_key = jax.random.fold_in(key, 0)
    drawn = jnp.clip(jax.random.normal(noise_key, (TOKENS, D), jnp.float32), -4.0, 4.0) * 2.5
    return drawn.astype(jnp.bfloat16)


def draw_key_value(key, part):
    key = jax.random.fold_in(key, 14)
    noise_key = jax.random.fold_in(key, 0)
    drawn = jnp.clip(jax.random.normal(noise_key, (TOKENS, 2, KV_COLS), jnp.float32), -4.0, 4.0)
    return drawn.astype(jnp.bfloat16)


def draw_span_mask(key, part):
    key = jax.random.fold_in(key, 12)
    row_ids = jnp.arange(SPANS, dtype=jnp.int32)[:, None]
    col_ids = jnp.arange(SPANS, dtype=jnp.int32)[None, :]
    drawn = jax.random.randint(key, (SPANS, SPANS), 0, 2, dtype=jnp.int32)
    nearby = (col_ids == row_ids) | (col_ids == row_ids - 1)
    return jnp.where(nearby, 1, jnp.where(col_ids < row_ids, drawn, 0)).astype(jnp.int32)


def draw_counts(key, part):
    key = jax.random.fold_in(key, 13)
    first_key, second_key, third_key = jax.random.split(key, 3)
    drawn = jax.random.randint(first_key, (SPANS,), SPAN_TOKENS // 2, SPAN_TOKENS + 1, dtype=jnp.int32)
    full_id = jax.random.randint(second_key, (), 0, SPANS, dtype=jnp.int32)
    half_id = (full_id + 1 + jax.random.randint(third_key, (), 0, SPANS - 1, dtype=jnp.int32)) % SPANS
    span_ids = jnp.arange(SPANS, dtype=jnp.int32)
    drawn = jnp.where(span_ids == half_id, SPAN_TOKENS // 2, drawn)
    return jnp.where(span_ids == full_id, SPAN_TOKENS, drawn).astype(jnp.int32)


def place_ends(values, own_key, low, top_value):
    place = [jax.random.randint(jax.random.fold_in(own_key, axis), (), 0, length) for axis, length in enumerate(values.shape)]
    widest = values.shape.index(max(values.shape))
    neighbour = place[:widest] + [(place[widest] + 1) % values.shape[widest]] + place[widest + 1:]
    return values.at[tuple(place)].set(low).at[tuple(neighbour)].set(top_value)


def block_scale(rng, shape, pieces, smallest, top_value):
    def one(dim, parts):
        draws = jax.random.uniform(jax.random.fold_in(jax.random.fold_in(rng, 6), dim), (parts,), jnp.float32, smallest / len(pieces), top_value / len(pieces))
        return jnp.repeat(jnp.exp(draws), shape[dim] // parts).reshape((-1,) + (1,) * (len(shape) - dim - 1))

    loudness = one(*pieces[0])
    for cut in pieces[1:]:
        loudness = loudness * one(*cut)
    return loudness


def noise(key, shape, deviation, most, cuts=(), kind=jnp.bfloat16):
    factor_of = block_scale(key, shape, cuts, -0.22, 0.18) if cuts else 1.0
    result = jax.random.normal(key, shape, jnp.float32) * deviation * factor_of
    return jnp.minimum(jnp.maximum(result, -most), most).astype(kind)


def setup_inputs(seed: int = 0, part: int = 0) -> dict:
    keys = jax.random.split(jax.random.key(seed), 8)
    part_splits = jax.random.split(jax.random.fold_in(keys[7], part), 8)
    return {
        "queries": draw_queries(jax.random.fold_in(jax.random.fold_in(keys[7], part), 71), part),
        "key_value": draw_key_value(jax.random.fold_in(jax.random.fold_in(keys[7], part), 71), part),
        "w_out": noise(keys[2], (D, D), D ** -0.5, 0.078125, ((0, 16),)),
        "gate_table": jnp.clip(jax.random.uniform(keys[3], (LEVELS, D), jnp.float32, 0.25, 2.0), 0.25, 2.0).astype(jnp.bfloat16),
        "levels": place_ends(jax.random.randint(part_splits[4], (SPANS,), 0, LEVELS), jax.random.fold_in(part_splits[4], 1), 0, LEVELS - 1).astype(jnp.int32),
        "span_mask": draw_span_mask(jax.random.fold_in(jax.random.fold_in(keys[7], part), 71), part),
        "counts": draw_counts(jax.random.fold_in(jax.random.fold_in(keys[7], part), 71), part),
    }


NEG_FILL = -1e30


def reference(queries, key_value, w_out, gate_table, levels, span_mask, counts):
    score_scale = HD ** -0.5
    share = HEADS // KV_GROUPS
    token_ids = jnp.arange(TOKENS, dtype=jnp.int32)
    key_span = token_ids // SPAN_TOKENS
    key_pos = token_ids % SPAN_TOKENS
    key_limit = counts[key_span]
    key_rows = key_value[:, 0].reshape(TOKENS, KV_GROUPS, HD).transpose(1, 0, 2)
    value_rows = key_value[:, 1].reshape(TOKENS, KV_GROUPS, HD).transpose(1, 0, 2)
    group = D // N_HEAD
    head_ids = jnp.arange(HEADS, dtype=jnp.int32)
    outputs = []
    for source in range(SPANS):
        usable = (span_mask[source][key_span] > 0) & (key_pos < key_limit)
        query_block = queries[source * SPAN_TOKENS:(source + 1) * SPAN_TOKENS]
        query_block = query_block.reshape(SPAN_TOKENS, HEADS, HD).transpose(1, 0, 2)

        def one_head(operands):
            query, head_id = operands
            keyset = key_rows[head_id // share]
            valueset = value_rows[head_id // share]
            scores = jnp.dot(query, keyset.T, preferred_element_type=jnp.float32) * score_scale
            scores = jnp.where(usable[None, :], scores, NEG_FILL)
            highest = jnp.max(scores, axis=1, keepdims=True)
            weights = jnp.where(usable[None, :], jnp.exp(scores - highest), 0.0)
            totals = jnp.sum(weights, axis=1, keepdims=True)
            summed = jnp.dot(weights.astype(jnp.bfloat16), valueset, preferred_element_type=jnp.float32)
            return summed / totals

        attended = lax.map(one_head, (query_block, head_ids))
        attended = attended.transpose(1, 0, 2).reshape(SPAN_TOKENS, D).astype(jnp.bfloat16)
        projected = jnp.zeros((SPAN_TOKENS, D), jnp.float32)
        for shard in range(N_HEAD):
            partial_value = jnp.dot(attended[:, shard * group:(shard + 1) * group],
                              w_out[shard * group:(shard + 1) * group],
                              preferred_element_type=jnp.float32)
            projected = projected + lax.optimization_barrier(partial_value.astype(jnp.bfloat16)).astype(jnp.float32)
        gate_row = gate_table[levels[source]].astype(jnp.float32)
        live = jnp.arange(SPAN_TOKENS, dtype=jnp.int32) < counts[source]
        outputs.append(jnp.where(live[:, None], projected * gate_row[None, :], 0.0).astype(jnp.bfloat16))
    return jnp.concatenate(outputs, axis=0)
```

```python
import jax
import jax.numpy as jnp
from jax import lax
from jax.experimental import pallas as pl
from jax.experimental.pallas import tpu as pltpu
from jax.sharding import PartitionSpec as P

MESH = pl.DeviceIdType.MESH
HD = 128
SPAN = 1024
D = 6144
ROWS = 64
QT = 256
SHARD = 384
ZC = 1024
QC = 1280
EXP_SCALE = HD**-0.5 * 1.4426950408889634
F32 = jnp.float32
BF16 = jnp.bfloat16


class Names:
    def __init__(self):
        self.ids = {}

    def __call__(self, name):
        return self.ids.setdefault(name, len(self.ids))


N_MESSAGES = 100
N_LOCAL = 8


def kernel(
    q_hbm, kv_hbm, w_hbm, gate_ref, levels_ref, mask_ref, counts_ref, out_ref,
    q_buf, kv_buf, kp, ve, m_ref, acc, a_st, a_buf, w_buf, o_st, ra_l, ra_r, rb_l, rb_r,
    gate_row, send_sem, recv_sem, local_sem,
):
    span = lax.axis_index("span")
    head = lax.axis_index("head")
    y = lax.axis_index("rep")
    core = lax.rem(span, 2)
    zl = head // 4
    x = lax.rem(head, 4)
    z = (span // 2) * 4 + zl
    a = x // 2
    b = lax.rem(x, 2)

    def at_x(xx):
        return {"head": zl * 4 + xx}

    def at_z(zz):
        return {"span": (zz // 4) * 2 + core, "head": lax.rem(zz, 4) * 4 + x}

    def at_y(yy):
        return {"rep": yy}

    sibling = {"span": (span // 2) * 2 + 1 - core}
    x_peers = [lax.rem(x + d, 4) for d in range(4)]
    z_right, z_left = lax.rem(z + 1, 8), lax.rem(z + 7, 8)
    y_right, y_left = lax.rem(y + 1, 4), lax.rem(y + 3, 4)
    y_far = lax.rem(y + 2, 4)

    names = Names()
    sent = []

    def message(name, src, dst, where):
        number = names(name)
        return pltpu.make_async_remote_copy(
            src_ref=src, dst_ref=dst, send_sem=send_sem.at[number], recv_sem=recv_sem.at[number],
            device_id=where, device_id_type=MESH,
        )

    def send(name, src, dst, where):
        message(name, src(), dst(), where()).start()
        sent.append((name, src, dst, where))

    def arrived(name, dst):
        message(name, dst, dst, sibling).wait_recv()

    barrier = pltpu.get_barrier_semaphore()
    peers = [at_x(x_peers[d]) for d in (1, 2, 3)]
    peers += [at_z(z_right), at_z(z_left), at_y(y_right), at_y(y_left), sibling]
    for peer in peers:
        pl.semaphore_signal(barrier, inc=1, device_id=peer, device_id_type=MESH)
    pl.semaphore_wait(barrier, len(peers))

    def group_of(xx, g):
        return 4 * lax.rem(xx, 2) + 2 * g + xx // 2

    def cols(start, width):
        return pl.ds(pl.multiple_of(start, 128), width)

    def rows(start, width):
        return pl.ds(pl.multiple_of(start, 64), width)

    def z_cols():
        return cols(core * (ZC // 2), ZC // 2)

    def q_cols(n):
        return cols(ZC + n * QC + core * (QC // 2), QC // 2)

    def z_cols_sib():
        return cols((1 - core) * (ZC // 2), ZC // 2)

    def q_cols_sib(n):
        return cols(ZC + n * QC + (1 - core) * (QC // 2), QC // 2)

    GROUPS = {"G1": (SHARD, 2 * SHARD), "G2": (3 * SHARD, SHARD)}

    def w_at(start, size, where):
        return w_buf.at[pl.ds(start, size), where()]

    def w_first(kind, where):
        send(kind + "R1", lambda: w_hbm.at[:, where()], lambda: w_at(SHARD, SHARD, where), lambda: at_z(z_right))
        send(kind + "L1", lambda: w_hbm.at[:, where()], lambda: w_at(2 * SHARD, SHARD, where), lambda: at_z(z_left))

    half = SHARD // 2

    def w_second(kind, where):
        arrived(kind + "R1", w_at(SHARD, SHARD, where))
        send(kind + "R2", lambda: w_at(SHARD, half, where), lambda: w_at(3 * SHARD, half, where), lambda: at_z(z_right))
        arrived(kind + "L1", w_at(2 * SHARD, SHARD, where))
        send(kind + "L2", lambda: w_at(2 * SHARD + half, half, where), lambda: w_at(3 * SHARD + half, half, where), lambda: at_z(z_left))

    def w_third(kind, where):
        arrived(kind + "R2", w_at(3 * SHARD, half, where))
        arrived(kind + "L2", w_at(3 * SHARD + half, half, where))

    def w_sibling(name, group, where):
        start, size = GROUPS[group]
        send("S" + name + group, lambda: w_at(start, size, where), lambda: w_at(start, size, where), lambda: sibling)

    def w_from_sibling(name, group, where):
        start, size = GROUPS[group]
        arrived("S" + name + group, w_at(start, size, where))

    def y_first(group):
        start, size = GROUPS[group]
        piece = lambda: w_at(start, size, lambda: q_cols(y))
        send("YR1" + group, piece, piece, lambda: at_y(y_right))
        send("YL1" + group, piece, piece, lambda: at_y(y_left))

    def y_second(group):
        start, size = GROUPS[group]
        part = size // 2
        arrived("YR1" + group, w_at(start, size, lambda: q_cols(y_left)))
        piece = lambda: w_at(start, part, lambda: q_cols(y_left))
        send("YR2" + group, piece, piece, lambda: at_y(y_right))
        w_sibling("ya", group, lambda: q_cols(y_left))
        arrived("YL1" + group, w_at(start, size, lambda: q_cols(y_right)))
        other = lambda: w_at(start + part, part, lambda: q_cols(y_right))
        send("YL2" + group, other, other, lambda: at_y(y_left))
        w_sibling("yb", group, lambda: q_cols(y_right))

    def y_third(group):
        start, size = GROUPS[group]
        part = size // 2
        arrived("YR2" + group, w_at(start, part, lambda: q_cols(y_far)))
        arrived("YL2" + group, w_at(start + part, part, lambda: q_cols(y_far)))
        w_sibling("yc", group, lambda: q_cols(y_far))

    def kv_sibling(slot):
        send("KS%d" % slot, lambda: kv_buf.at[slot, 0], lambda: kv_buf.at[slot, 1], lambda: sibling)

    def kv_from_sibling(slot):
        arrived("KS%d" % slot, kv_buf.at[slot, 1])

    def kv_step(step):
        from_left, from_right = 2 * step - 1, 2 * step
        arrived("KR%d" % step, kv_buf.at[from_left, 0])
        arrived("KL%d" % step, kv_buf.at[from_right, 0])
        if step < 3:
            send("KR%d" % (step + 1), lambda: kv_buf.at[from_left, 0], lambda: kv_buf.at[from_left + 2, 0], lambda: at_z(z_right))
            send("KL%d" % (step + 1), lambda: kv_buf.at[from_right, 0], lambda: kv_buf.at[from_right + 2, 0], lambda: at_z(z_left))
        else:
            send("KR4", lambda: kv_buf.at[5, 0, 0], lambda: kv_buf.at[7, 0, 0], lambda: at_z(z_right))
            send("KL4", lambda: kv_buf.at[6, 0, 1], lambda: kv_buf.at[7, 0, 1], lambda: at_z(z_left))
        kv_sibling(from_left)
        kv_sibling(from_right)

    def kv_last():
        arrived("KR4", kv_buf.at[7, 0, 0])
        arrived("KL4", kv_buf.at[7, 0, 1])
        kv_sibling(7)

    def local_copy(number, src, dst):
        copy = pltpu.make_async_copy(src, dst, local_sem.at[number])
        copy.start()
        return copy

    def kv_across(d, g):
        send(
            "KX%d%d" % (d, g),
            lambda: kv_hbm.at[:, :, cols(group_of(x_peers[d], g) * HD, HD)],
            lambda: kv_buf.at[0, 0, g, :, rows(x * ROWS, ROWS), :],
            lambda: at_x(x_peers[d]),
        )

    def q_across(d, g):
        send(
            "QX%d%d" % (d, g),
            lambda: q_hbm.at[:, cols(group_of(x_peers[d], g) * 768, 768)],
            lambda: q_buf.at[g, rows(x * ROWS, ROWS), :],
            lambda: at_x(x_peers[d]),
        )

    for d in (1, 3, 2):
        for g in range(2):
            kv_across(d, g)
    kv_local = [
        local_copy(g, kv_hbm.at[:, :, cols(group_of(x, g) * HD, HD)], kv_buf.at[0, 0, g, :, rows(x * ROWS, ROWS), :])
        for g in range(2)
    ]
    w_first("Q", lambda: q_cols(y))
    for d in (1, 3, 2):
        for g in range(2):
            q_across(d, g)
    q_local = [
        local_copy(2 + g, q_hbm.at[:, cols(group_of(x, g) * 768, 768)], q_buf.at[g, rows(x * ROWS, ROWS), :])
        for g in range(2)
    ]
    w_local = local_copy(4, w_hbm, w_buf.at[pl.ds(0, SHARD), :])

    for copy in kv_local:
        copy.wait()
    for d in (1, 3, 2):
        for g in range(2):
            arrived("KX%d%d" % (d, g), kv_buf.at[0, 0, g, :, rows(x_peers[4 - d] * ROWS, ROWS), :])
    send("KR1", lambda: kv_buf.at[0, 0], lambda: kv_buf.at[1, 0], lambda: at_z(z_right))
    send("KL1", lambda: kv_buf.at[0, 0], lambda: kv_buf.at[2, 0], lambda: at_z(z_left))
    kv_sibling(0)

    m_ref[...] = jnp.full(m_ref.shape, -1e30, F32)
    acc[...] = jnp.zeros(acc.shape, F32)
    chosen = (lax.broadcasted_iota(jnp.int32, (16, 64), 1) == levels_ref[span]).astype(F32).astype(BF16)
    for part in range(4):
        where = pl.ds(part * 1536, 1536)
        gate_row[:, where] = jnp.dot(chosen, gate_ref[:, where], preferred_element_type=F32)

    for copy in q_local:
        copy.wait()
    for d in (1, 3, 2):
        for g in range(2):
            arrived("QX%d%d" % (d, g), q_buf.at[g, rows(x_peers[4 - d] * ROWS, ROWS), :])
    kv_step(1)

    def prepare(tile):
        for slot in (2 * tile, 2 * tile + 1):
            step = (slot + 1) // 2
            src_z = lax.rem(z + (8 - step if slot % 2 else step), 8)
            for rel in range(2):
                src_span = (src_z // 4) * 2 + (core if rel == 0 else 1 - core)
                limit = counts_ref[src_span] * mask_ref[span, src_span]
                place = lax.broadcasted_iota(jnp.int32, (QT, HD), 0) + lax.rem(src_z, 4) * QT
                keep = jnp.where(place < limit, 1.0, 0.0).astype(BF16)
                drop = jnp.where(place < limit, 0.0, 1.0).astype(BF16)
                at = pl.ds((slot - 2 * tile) * 512 + rel * 256, QT)
                for g in range(2):
                    stand_in = jnp.broadcast_to(kv_buf[0, 0, g, 0, 0:16, :].astype(F32)[0:1], (QT, HD)).astype(BF16)
                    kp[g, at, :] = kv_buf[slot, rel, g, 0] * keep + stand_in * drop
                    ve[g, at, 0:HD] = kv_buf[slot, rel, g, 1] * keep
                    ve[g, at, HD : 2 * HD] = keep

    def a_place(g):
        d = lax.rem(2 * b + g - zl + 8, 4)
        slot = (lax.rem(d, 3) + 1) * jnp.minimum(d, 1)
        return a_buf.at[:, cols(slot * SHARD, SHARD)]

    def a_place_from(g):
        d = lax.rem(2 * (1 - b) + g - zl + 8, 4)
        slot = (lax.rem(d, 3) + 1) * jnp.minimum(d, 1)
        return a_buf.at[:, cols(slot * SHARD, SHARD)]

    partner = at_x(x + 1 - 2 * b)

    def a_out(g):
        send("A%d" % g, lambda: a_st.at[g, 1 - b], lambda: a_place(g), lambda: partner)

    def a_own(g):
        local_copy(5 + g, a_st.at[g, b], a_place(g))

    def service(i):
        todo = {
            0: lambda: (kv_from_sibling(0), kv_from_sibling(1), prepare(0)),
            1: lambda: (w_second("Q", lambda: q_cols(y)), y_first("G1"), w_sibling("q", "G1", lambda: q_cols(y))),
            2: lambda: kv_step(2),
            3: lambda: w_first("Z", z_cols),
            4: lambda: (kv_from_sibling(2), kv_from_sibling(3), prepare(1)),
            5: lambda: (w_third("Q", lambda: q_cols(y)), y_first("G2"), w_sibling("q", "G2", lambda: q_cols(y))),
            6: lambda: kv_step(3),
            8: lambda: (kv_from_sibling(4), kv_from_sibling(5), prepare(2)),
            10: lambda: kv_last(),
            11: lambda: (w_second("Z", z_cols), w_sibling("z", "G1", z_cols)),
            12: lambda: (kv_from_sibling(6), kv_from_sibling(7), prepare(3)),
            14: lambda: (w_third("Z", z_cols), w_sibling("z", "G2", z_cols)),
        }
        for when, what in todo.items():
            pl.when(i == when)(lambda what=what: (what(), None)[1])

    def attend(i, carry):
        service(i)
        g = lax.rem(i // 2, 2)
        side = lax.rem(1 - b + lax.rem(i, 2), 2)
        for j in range(3):
            h = side * 3 + j
            query = q_buf[g, :, cols(h * HD, HD)]
            scores = lax.dot_general(query, kp[g], (((1,), (1,)), ((), ())), preferred_element_type=F32)
            earlier = m_ref[g, h]
            latest = jnp.maximum(earlier, jnp.max(scores, axis=1, keepdims=True))
            weights = jnp.exp2((scores - latest[:, 0:1]) * EXP_SCALE).astype(BF16)
            factor = jnp.exp2((earlier - latest) * EXP_SCALE)
            both = jnp.dot(weights, ve[g], preferred_element_type=F32)
            m_ref[g, h] = latest
            acc[g, h, :, 0:HD] = acc[g, h, :, 0:HD] * factor + both[:, 0:HD]
            acc[g, h, :, HD : 2 * HD] = acc[g, h, :, HD : 2 * HD] * factor + both[:, HD : 2 * HD]

        @pl.when(i >= 12)
        def _():
            for j in range(3):
                h = side * 3 + j
                a_st[g, side, :, j * HD : (j + 1) * HD] = (acc[g, h, :, 0:HD] / acc[g, h, :, HD : 2 * HD]).astype(BF16)

        for when, what in {12: lambda: a_out(0), 13: lambda: a_own(0), 14: lambda: a_out(1), 15: lambda: a_own(1)}.items():
            pl.when(i == when)(what)
        return carry

    lax.fori_loop(0, 16, attend, 0)

    for g in range(2):
        pltpu.make_async_copy(a_st.at[g, b], a_place(g), local_sem.at[5 + g]).wait()
        arrived("A%d" % g, a_place_from(g))
    w_local.wait()

    order = [(0, ZC)] + [(ZC + n * QC, QC) for n in (y, y_left, y_right, y_far)]
    x_right, x_left, x_far = x_peers[1], x_peers[3], x_peers[2]

    def project(k):
        start, width = order[k]

        def piece(n, carry):
            part = jnp.dot(a_buf[...], w_buf[:, cols(start + n * 256, 256)], preferred_element_type=F32)
            o_st[k, :, cols(n * 256, 256)] = part.astype(BF16)
            return carry

        lax.fori_loop(0, width // 256, piece, 0)
        h = width // 2
        send("RA%d" % k, lambda: o_st.at[k, rows(x_far * ROWS, ROWS), pl.ds(0, h)], lambda: ra_l.at[k, :, pl.ds(0, h)], lambda: at_x(x_right))
        send("LA%d" % k, lambda: o_st.at[k, rows(x_far * ROWS, ROWS), pl.ds(h, h)], lambda: ra_r.at[k, :, pl.ds(0, h)], lambda: at_x(x_left))

    def pass_on(k):
        start, width = order[k]
        h = width // 2
        arrived("RA%d" % k, ra_l.at[k, :, pl.ds(0, h)])
        mine = o_st[k, rows(x_right * ROWS, ROWS), 0:h].astype(F32)
        o_st[k, rows(x_right * ROWS, ROWS), 0:h] = (mine + ra_l[k, :, 0:h].astype(F32)).astype(BF16)
        send("RB%d" % k, lambda: o_st.at[k, rows(x_right * ROWS, ROWS), pl.ds(0, width)], lambda: rb_l.at[k, :, pl.ds(0, width)], lambda: at_x(x_right))
        arrived("LA%d" % k, ra_r.at[k, :, pl.ds(0, h)])
        mine = o_st[k, rows(x_left * ROWS, ROWS), h:width].astype(F32)
        o_st[k, rows(x_left * ROWS, ROWS), h:width] = (mine + ra_r[k, :, 0:h].astype(F32)).astype(BF16)
        send("LB%d" % k, lambda: o_st.at[k, rows(x_left * ROWS, ROWS), pl.ds(0, width)], lambda: rb_r.at[k, :, pl.ds(0, width)], lambda: at_x(x_left))

    def finish(k):
        start, width = order[k]
        arrived("RB%d" % k, rb_l.at[k, :, pl.ds(0, width)])
        arrived("LB%d" % k, rb_r.at[k, :, pl.ds(0, width)])
        total = o_st[k, rows(x * ROWS, ROWS), 0:width].astype(F32)
        total = total + rb_l[k, :, 0:width].astype(F32) + rb_r[k, :, 0:width].astype(F32)
        place = lax.broadcasted_iota(jnp.int32, (ROWS, width), 0) + head * ROWS
        gated = total * gate_row[0:1, cols(start, width)]
        out_ref[:, cols(start, width)] = jnp.where(place < counts_ref[span], gated, 0.0).astype(BF16)

    w_from_sibling("z", "G1", z_cols_sib)
    w_from_sibling("z", "G2", z_cols_sib)
    project(0)
    w_from_sibling("q", "G1", lambda: q_cols_sib(y))
    w_from_sibling("q", "G2", lambda: q_cols_sib(y))
    project(1)
    y_second("G1")
    pass_on(0)
    y_second("G2")
    pass_on(1)
    for group in GROUPS:
        w_from_sibling("ya", group, lambda: q_cols_sib(y_left))
    project(2)
    for group in GROUPS:
        w_from_sibling("yb", group, lambda: q_cols_sib(y_right))
    project(3)
    finish(0)
    pass_on(2)
    pass_on(3)
    y_third("G1")
    y_third("G2")
    for group in GROUPS:
        w_from_sibling("yc", group, lambda: q_cols_sib(y_far))
    project(4)
    finish(1)
    finish(2)
    pass_on(4)
    finish(3)
    finish(4)
    for name, src, dst, where in sent:
        message(name, src(), dst(), where()).wait_send()


def local(queries, key_value, w_out, gate_table, levels, span_mask, counts):
    kv = jnp.transpose(key_value, (1, 0, 2))
    anywhere = pl.BlockSpec(memory_space=pl.ANY)
    vmem = pl.BlockSpec(memory_space=pltpu.VMEM)
    smem = pl.BlockSpec(memory_space=pltpu.SMEM)
    return pl.pallas_call(
        kernel,
        out_shape=jax.ShapeDtypeStruct((ROWS, D), BF16),
        in_specs=[anywhere, anywhere, anywhere, vmem, smem, smem, smem],
        out_specs=vmem,
        scratch_shapes=[
            pltpu.VMEM((2, QT, 768), BF16),
            pltpu.VMEM((8, 2, 2, 2, QT, HD), BF16),
            pltpu.VMEM((2, 1024, HD), BF16),
            pltpu.VMEM((2, 1024, 2 * HD), BF16),
            pltpu.VMEM((2, 6, QT, HD), F32),
            pltpu.VMEM((2, 6, QT, 2 * HD), F32),
            pltpu.VMEM((2, 2, QT, SHARD), BF16),
            pltpu.VMEM((QT, 4 * SHARD), BF16),
            pltpu.VMEM((4 * SHARD, D), BF16),
            pltpu.VMEM((5, QT, QC), BF16),
            pltpu.VMEM((5, ROWS, QC // 2), BF16),
            pltpu.VMEM((5, ROWS, QC // 2), BF16),
            pltpu.VMEM((5, ROWS, QC), BF16),
            pltpu.VMEM((5, ROWS, QC), BF16),
            pltpu.VMEM((16, D), F32),
            pltpu.SemaphoreType.DMA((N_MESSAGES,)),
            pltpu.SemaphoreType.DMA((N_MESSAGES,)),
            pltpu.SemaphoreType.DMA((N_LOCAL,)),
        ],
        compiler_params=pltpu.CompilerParams(
            collective_id=0, has_side_effects=True, vmem_limit_bytes=56 * 1024 * 1024
        ),
    )(queries, kv, w_out, gate_table, levels, span_mask, counts)


def solution(mesh):
    in_specs = (
        P(("rep", "span", "head"), None),
        P(("rep", "span", "head"), None, None),
        P("head", None),
        P(),
        P("rep"),
        P("rep", None),
        P("rep"),
    )
    out_specs = P(("rep", "span", "head"), None)
    return jax.shard_map(local, mesh=mesh, in_specs=in_specs, out_specs=out_specs, check_vma=False)
```

```python
import jax
import jax.numpy as jnp
from jax import lax
from jax.experimental import pallas as pl
from jax.experimental.pallas import tpu as pltpu
from jax.sharding import PartitionSpec as P

MESH = pl.DeviceIdType.MESH
HD = 128
SPAN = 1024
D = 6144
ROWS = 64
QT = 256
SHARD = 384
NC = 3072
QC = 768
EXP_SCALE = HD**-0.5 * 1.4426950408889634
F32 = jnp.float32
BF16 = jnp.bfloat16


class Names:
    def __init__(self):
        self.ids = {}

    def __call__(self, name):
        return self.ids.setdefault(name, len(self.ids))


N_MESSAGES = 130
N_LOCAL = 8


def kernel(
    q_hbm, kv_hbm, w_hbm, gate_ref, levels_ref, mask_ref, counts_ref, out_ref,
    q_buf, kv_buf, kp, ve, m_ref, acc, a_st, a_buf, w_buf, o_st, ra_l, ra_r, rb_l, rb_r,
    f_out, f_in, gate_row, send_sem, recv_sem, local_sem,
):
    span = lax.axis_index("span")
    head = lax.axis_index("head")
    y = lax.axis_index("rep")
    core = lax.rem(span, 2)
    zl = head // 4
    x = lax.rem(head, 4)
    z = (span // 2) * 4 + zl
    a = x // 2
    b = lax.rem(x, 2)

    def at_x(xx):
        return {"head": zl * 4 + xx}

    def at_z(zz):
        return {"span": (zz // 4) * 2 + core, "head": lax.rem(zz, 4) * 4 + x}

    def at_y(yy):
        return {"rep": yy}

    sibling = {"span": (span // 2) * 2 + 1 - core}
    x_peers = [lax.rem(x + d, 4) for d in range(4)]
    z_right, z_left = lax.rem(z + 1, 8), lax.rem(z + 7, 8)
    y_right, y_left = lax.rem(y + 1, 4), lax.rem(y + 3, 4)
    y_far = lax.rem(y + 2, 4)
    z_right2, z_left2 = lax.rem(z + 2, 8), lax.rem(z + 6, 8)
    parity = lax.rem(z, 2)
    z_pair = z + 1 - 2 * parity

    names = Names()
    sent = []

    def message(name, src, dst, where):
        number = names(name)
        return pltpu.make_async_remote_copy(
            src_ref=src, dst_ref=dst, send_sem=send_sem.at[number], recv_sem=recv_sem.at[number],
            device_id=where, device_id_type=MESH,
        )

    def send(name, src, dst, where):
        message(name, src(), dst(), where()).start()
        sent.append((name, src, dst, where))

    def arrived(name, dst):
        message(name, dst, dst, sibling).wait_recv()

    barrier = pltpu.get_barrier_semaphore()
    peers = [at_x(x_peers[d]) for d in (1, 2, 3)]
    peers += [at_z(zz) for zz in (z_right, z_left, z_right2, z_left2)]
    peers += [at_y(yy) for yy in (y_right, y_left, y_far)]
    peers += [sibling]
    for peer in peers:
        pl.semaphore_signal(barrier, inc=1, device_id=peer, device_id_type=MESH)
    pl.semaphore_wait(barrier, len(peers))

    def group_of(xx, g):
        return 4 * lax.rem(xx, 2) + 2 * g + xx // 2

    def cols(start, width):
        return pl.ds(pl.multiple_of(start, 128), width)

    def rows(start, width):
        return pl.ds(pl.multiple_of(start, 64), width)

    half = SHARD // 2
    WIDE = QC // 2

    def q_cols(n, of_core=None):
        return cols(n * QC + (core if of_core is None else of_core) * WIDE, WIDE)

    def w_own(start, size, side):
        return w_hbm.at[pl.ds(start, size), cols(side * NC + y * QC + core * WIDE, WIDE)]

    def w_at(start, size, n, of_core=None):
        return w_buf.at[pl.ds(start, size), q_cols(n, of_core)]

    def w_near():
        send("WR1", lambda: w_own(0, SHARD, 1 - parity), lambda: w_at(SHARD, SHARD, y), lambda: at_z(z_right))
        send("WL1", lambda: w_own(0, SHARD, 1 - parity), lambda: w_at(2 * SHARD, SHARD, y), lambda: at_z(z_left))

    def w_far():
        send("WR2", lambda: w_own(0, half, parity), lambda: w_at(3 * SHARD, half, y), lambda: at_z(z_right2))
        send("WL2", lambda: w_own(half, half, parity), lambda: w_at(3 * SHARD + half, half, y), lambda: at_z(z_left2))

    def y_out(slot):
        send("YR%d" % slot, lambda: w_at(slot * SHARD, SHARD, y), lambda: w_at(slot * SHARD, SHARD, y), lambda: at_y(y_right))
        send("YL%d" % slot, lambda: w_at(slot * SHARD, SHARD, y), lambda: w_at(slot * SHARD, SHARD, y), lambda: at_y(y_left))
        send("YF%d" % slot, lambda: w_at(slot * SHARD, SHARD, y), lambda: w_at(slot * SHARD, SHARD, y), lambda: at_y(y_far))

    def w_got_near():
        arrived("WR1", w_at(SHARD, SHARD, y))
        y_out(1)
        arrived("WL1", w_at(2 * SHARD, SHARD, y))
        y_out(2)

    def w_sibling(name, n):
        send("S" + name, lambda: w_at(SHARD, 3 * SHARD, n), lambda: w_at(SHARD, 3 * SHARD, n), lambda: sibling)

    def w_from_sibling(name, n):
        arrived("S" + name, w_at(SHARD, 3 * SHARD, n, 1 - core))

    def w_got_far():
        arrived("WR2", w_at(3 * SHARD, half, y))
        arrived("WL2", w_at(3 * SHARD + half, half, y))
        y_out(3)
        w_sibling("YO", y)

    def y_got(way, n):
        for slot in (1, 2, 3):
            arrived("%s%d" % (way, slot), w_at(slot * SHARD, SHARD, n))
        w_sibling(way, n)

    def kv_sibling(slot, g):
        send("KS%d%d" % (slot, g), lambda: kv_buf.at[slot, 0, g], lambda: kv_buf.at[slot, 1, g], lambda: sibling)

    def kv_from_sibling(slot, g):
        arrived("KS%d%d" % (slot, g), kv_buf.at[slot, 1, g])

    def kv_send(step, from_slot, g, right):
        to_slot = 2 * step - 1 if right else 2 * step
        if step == 4:
            to_slot = 7
        send(
            ("KR%d%d" if right else "KL%d%d") % (step, g),
            lambda: kv_buf.at[from_slot, 0, g],
            lambda: kv_buf.at[to_slot, 0, g],
            lambda: at_z(z_right if right else z_left),
        )

    def kv_step(step, g):
        from_left, from_right = 2 * step - 1, 2 * step
        arrived("KR%d%d" % (step, g), kv_buf.at[from_left, 0, g])
        if step < 3 or g == 0:
            kv_send(step + 1, from_left, g, True)
        arrived("KL%d%d" % (step, g), kv_buf.at[from_right, 0, g])
        if step < 3 or g == 1:
            kv_send(step + 1, from_right, g, False)
        kv_sibling(from_left, g)
        kv_sibling(from_right, g)

    def kv_last():
        arrived("KR40", kv_buf.at[7, 0, 0])
        kv_sibling(7, 0)
        arrived("KL41", kv_buf.at[7, 0, 1])
        kv_sibling(7, 1)

    def local_copy(number, src, dst):
        copy = pltpu.make_async_copy(src, dst, local_sem.at[number])
        copy.start()
        return copy

    def kv_across(d, g):
        send(
            "KX%d%d" % (d, g),
            lambda: kv_hbm.at[:, :, cols(group_of(x_peers[d], g) * HD, HD)],
            lambda: kv_buf.at[0, 0, g, :, rows(x * ROWS, ROWS), :],
            lambda: at_x(x_peers[d]),
        )

    def q_across(d, g):
        send(
            "QX%d%d" % (d, g),
            lambda: q_hbm.at[:, cols(group_of(x_peers[d], g) * 768, 768)],
            lambda: q_buf.at[g, rows(x * ROWS, ROWS), :],
            lambda: at_x(x_peers[d]),
        )

    for g in range(2):
        for d in (1, 3, 2):
            kv_across(d, g)
    kv_local = [
        local_copy(g, kv_hbm.at[:, :, cols(group_of(x, g) * HD, HD)], kv_buf.at[0, 0, g, :, rows(x * ROWS, ROWS), :])
        for g in range(2)
    ]
    w_near()
    for d in (1, 3, 2):
        for g in range(2):
            q_across(d, g)
    q_local = [
        local_copy(2 + g, q_hbm.at[:, cols(group_of(x, g) * 768, 768)], q_buf.at[g, rows(x * ROWS, ROWS), :])
        for g in range(2)
    ]
    w_local = local_copy(4, w_hbm.at[:, cols(parity * NC, NC)], w_buf.at[pl.ds(0, SHARD), :])

    m_ref[...] = jnp.full(m_ref.shape, -1e30, F32)
    acc[...] = jnp.zeros(acc.shape, F32)

    for g in range(2):
        kv_local[g].wait()
        for d in (1, 3, 2):
            arrived("KX%d%d" % (d, g), kv_buf.at[0, 0, g, :, rows(x_peers[4 - d] * ROWS, ROWS), :])
        kv_send(1, 0, g, True)
        kv_send(1, 0, g, False)
        kv_sibling(0, g)

    chosen = (lax.broadcasted_iota(jnp.int32, (16, 64), 1) == levels_ref[span]).astype(F32).astype(BF16)
    for part in range(2):
        gate_row[:, part * 1536 : (part + 1) * 1536] = jnp.dot(
            chosen, gate_ref[:, cols(parity * NC + part * 1536, 1536)], preferred_element_type=F32
        )

    kv_step(1, 0)
    w_got_near()
    kv_step(1, 1)
    for copy in q_local:
        copy.wait()
    for d in (1, 3, 2):
        for g in range(2):
            arrived("QX%d%d" % (d, g), q_buf.at[g, rows(x_peers[4 - d] * ROWS, ROWS), :])

    def prepare(tile, g):
        for slot in (2 * tile, 2 * tile + 1):
            kv_from_sibling(slot, g)
        for slot in (2 * tile, 2 * tile + 1):
            step = (slot + 1) // 2
            src_z = lax.rem(z + (8 - step if slot % 2 else step), 8)
            for rel in range(2):
                src_span = (src_z // 4) * 2 + (core if rel == 0 else 1 - core)
                limit = counts_ref[src_span] * mask_ref[span, src_span]
                place = lax.broadcasted_iota(jnp.int32, (QT, HD), 0) + lax.rem(src_z, 4) * QT
                keep = jnp.where(place < limit, 1.0, 0.0).astype(BF16)
                drop = jnp.where(place < limit, 0.0, 1.0).astype(BF16)
                at = pl.ds((slot - 2 * tile) * 512 + rel * 256, QT)
                stand_in = jnp.broadcast_to(kv_buf[0, 0, g, 0, 0:16, :].astype(F32)[0:1], (QT, HD)).astype(BF16)
                kp[g, at, :] = kv_buf[slot, rel, g, 0] * keep + stand_in * drop
                ve[g, at, 0:HD] = kv_buf[slot, rel, g, 1] * keep
                ve[g, at, HD : 2 * HD] = keep

    def a_place(place, shard, zz):
        d = lax.rem(shard - lax.rem(zz, 4) + 4, 4)
        slot = (lax.rem(d, 3) + 1) * jnp.minimum(d, 1)
        return a_buf.at[pl.ds(place * QT, QT), cols(slot * SHARD, SHARD)]

    partner = at_x(x + 1 - 2 * b)

    def a_across(g):
        send("AX%d" % g, lambda: a_st.at[g, 1 - b], lambda: a_place(0, 2 * b + g, z), lambda: partner)

    def a_own(g):
        local_copy(5 + g, a_st.at[g, b], a_place(0, 2 * b + g, z))
        send("AZ%d" % g, lambda: a_st.at[g, b], lambda: a_place(1, 2 * b + g, z_pair), lambda: at_z(z_pair))

    def a_forward(g):
        mine = lambda: a_place(0, 2 * (1 - b) + g, z)
        arrived("AX%d" % g, mine())
        send("AF%d" % g, mine, lambda: a_place(1, 2 * (1 - b) + g, z_pair), lambda: at_z(z_pair))

    def service(i):
        todo = {
            0: lambda: prepare(0, 0),
            1: lambda: prepare(0, 1),
            2: lambda: kv_step(2, 0),
            3: lambda: kv_step(2, 1),
            4: lambda: prepare(1, 0),
            5: lambda: prepare(1, 1),
            6: lambda: kv_step(3, 0),
            7: lambda: kv_step(3, 1),
            8: lambda: (prepare(2, 0), w_far()),
            9: lambda: prepare(2, 1),
            10: lambda: kv_last(),
            12: lambda: prepare(3, 0),
            13: lambda: prepare(3, 1),
            14: lambda: w_got_far(),
        }
        for when, what in todo.items():
            pl.when(i == when)(lambda what=what: (what(), None)[1])

    def attend(i, carry):
        service(i)
        g = lax.rem(i, 2)
        side = lax.rem(1 - b + lax.rem(i // 2, 2), 2)
        heads = [side * 3 + j for j in range(3)]
        keys, values = kp[g], ve[g]
        queries = [q_buf[g, :, cols(h * HD, HD)] for h in heads]
        earlier = [m_ref[g, h] for h in heads]
        sums = [acc[g, h] for h in heads]
        latest, results = [], []

        def score(j):
            return lax.dot_general(queries[j], keys, (((1,), (1,)), ((), ())), preferred_element_type=F32)

        ahead = score(0)
        for j in range(3):
            scores = ahead
            if j < 2:
                ahead = score(j + 1)
            top = jnp.maximum(earlier[j], jnp.max(scores, axis=1, keepdims=True))
            latest.append(top)
            weights = jnp.exp2((scores - jnp.concatenate([top] * 8, axis=1)) * EXP_SCALE).astype(BF16)
            factor = jnp.exp2((earlier[j] - top) * EXP_SCALE)
            both = jnp.dot(weights, values, preferred_element_type=F32)
            results.append(sums[j] * jnp.concatenate([factor] * 2, axis=1) + both)
        for j in range(3):
            m_ref[g, heads[j]] = latest[j]
            acc[g, heads[j]] = results[j]

        @pl.when(i >= 12)
        def _():
            for j in range(3):
                h = side * 3 + j
                a_st[g, side, :, j * HD : (j + 1) * HD] = (acc[g, h, :, 0:HD] / acc[g, h, :, HD : 2 * HD]).astype(BF16)

        for when, what in {12: lambda: a_across(0), 13: lambda: a_across(1), 14: lambda: a_own(0), 15: lambda: a_own(1)}.items():
            pl.when(i == when)(what)
        return carry

    lax.fori_loop(0, 16, attend, 0)

    for g in range(2):
        a_forward(g)
    for g in range(2):
        pltpu.make_async_copy(a_st.at[g, b], a_place(0, 2 * b + g, z), local_sem.at[5 + g]).wait()
    w_local.wait()

    quarters = [y, y_left, y_right, y_far]
    x_right, x_left, x_far = x_peers[1], x_peers[3], x_peers[2]
    width = QC

    def project(k):
        tokens = pl.ds((k // 4) * QT, QT)
        start = quarters[k % 4] * QC

        def piece(n, carry):
            part = jnp.dot(a_buf[tokens, :], w_buf[:, cols(start + n * 256, 256)], preferred_element_type=F32)
            o_st[k, :, cols(n * 256, 256)] = part.astype(BF16)
            return carry

        lax.fori_loop(0, width // 256, piece, 0)
        h = width // 2
        send("RA%d" % k, lambda: o_st.at[k, rows(x_far * ROWS, ROWS), pl.ds(0, h)], lambda: ra_l.at[k, :, pl.ds(0, h)], lambda: at_x(x_right))
        send("LA%d" % k, lambda: o_st.at[k, rows(x_far * ROWS, ROWS), pl.ds(h, h)], lambda: ra_r.at[k, :, pl.ds(0, h)], lambda: at_x(x_left))

    def pass_on(k):
        h = width // 2
        arrived("RA%d" % k, ra_l.at[k, :, pl.ds(0, h)])
        mine = o_st[k, rows(x_right * ROWS, ROWS), 0:h].astype(F32)
        o_st[k, rows(x_right * ROWS, ROWS), 0:h] = (mine + ra_l[k, :, 0:h].astype(F32)).astype(BF16)
        send("RB%d" % k, lambda: o_st.at[k, rows(x_right * ROWS, ROWS), pl.ds(0, width)], lambda: rb_l.at[k, :, pl.ds(0, width)], lambda: at_x(x_right))
        arrived("LA%d" % k, ra_r.at[k, :, pl.ds(0, h)])
        mine = o_st[k, rows(x_left * ROWS, ROWS), h:width].astype(F32)
        o_st[k, rows(x_left * ROWS, ROWS), h:width] = (mine + ra_r[k, :, 0:h].astype(F32)).astype(BF16)
        send("LB%d" % k, lambda: o_st.at[k, rows(x_left * ROWS, ROWS), pl.ds(0, width)], lambda: rb_r.at[k, :, pl.ds(0, width)], lambda: at_x(x_left))

    def finish(k):
        arrived("RB%d" % k, rb_l.at[k, :, pl.ds(0, width)])
        arrived("LB%d" % k, rb_r.at[k, :, pl.ds(0, width)])
        total = o_st[k, rows(x * ROWS, ROWS), 0:width].astype(F32)
        total = total + rb_l[k, :, 0:width].astype(F32) + rb_r[k, :, 0:width].astype(F32)
        n = quarters[k % 4]
        owner = head if k < 4 else lax.rem(z_pair, 4) * 4 + x
        place = lax.broadcasted_iota(jnp.int32, (ROWS, width), 0) + owner * ROWS
        gated = total * gate_row[0:1, cols(n * QC, QC)]
        result = jnp.where(place < counts_ref[span], gated, 0.0).astype(BF16)
        if k < 4:
            out_ref[:, cols(parity * NC + n * QC, QC)] = result
        else:
            f_out[k - 4] = result
            send("F%d" % (k - 4), lambda: f_out.at[k - 4], lambda: f_in.at[k - 4], lambda: at_z(z_pair))

    def take(k):
        arrived("F%d" % k, f_in.at[k])
        out_ref[:, cols((1 - parity) * NC + quarters[k] * QC, QC)] = f_in[k]

    w_from_sibling("YO", y)
    project(0)
    y_got("YR", y_left)
    y_got("YL", y_right)
    y_got("YF", y_far)
    w_from_sibling("YR", y_left)
    project(1)
    w_from_sibling("YL", y_right)
    project(2)
    pass_on(0)
    w_from_sibling("YF", y_far)
    pass_on(1)
    pass_on(2)
    for g in range(2):
        arrived("AZ%d" % g, a_place(1, 2 * b + g, z))
        arrived("AF%d" % g, a_place(1, 2 * (1 - b) + g, z))
    for k in (4, 5, 6, 7):
        project(k)
    pass_on(4)
    project(3)
    finish(0)
    pass_on(5)
    finish(1)
    pass_on(6)
    finish(2)
    pass_on(7)
    pass_on(3)
    for k in (4, 5, 6, 7):
        finish(k)
    for k in range(4):
        take(k)
    finish(3)
    for name, src, dst, where in sent:
        message(name, src(), dst(), where()).wait_send()


def local(queries, key_value, w_out, gate_table, levels, span_mask, counts):
    kv = jnp.transpose(key_value, (1, 0, 2))
    anywhere = pl.BlockSpec(memory_space=pl.ANY)
    vmem = pl.BlockSpec(memory_space=pltpu.VMEM)
    smem = pl.BlockSpec(memory_space=pltpu.SMEM)
    return pl.pallas_call(
        kernel,
        out_shape=jax.ShapeDtypeStruct((ROWS, D), BF16),
        in_specs=[anywhere, anywhere, anywhere, vmem, smem, smem, smem],
        out_specs=vmem,
        scratch_shapes=[
            pltpu.VMEM((2, QT, 768), BF16),
            pltpu.VMEM((8, 2, 2, 2, QT, HD), BF16),
            pltpu.VMEM((2, 1024, HD), BF16),
            pltpu.VMEM((2, 1024, 2 * HD), BF16),
            pltpu.VMEM((2, 6, QT, HD), F32),
            pltpu.VMEM((2, 6, QT, 2 * HD), F32),
            pltpu.VMEM((2, 2, QT, SHARD), BF16),
            pltpu.VMEM((2 * QT, 4 * SHARD), BF16),
            pltpu.VMEM((4 * SHARD, NC), BF16),
            pltpu.VMEM((8, QT, QC), BF16),
            pltpu.VMEM((8, ROWS, QC // 2), BF16),
            pltpu.VMEM((8, ROWS, QC // 2), BF16),
            pltpu.VMEM((8, ROWS, QC), BF16),
            pltpu.VMEM((8, ROWS, QC), BF16),
            pltpu.VMEM((4, ROWS, QC), BF16),
            pltpu.VMEM((4, ROWS, QC), BF16),
            pltpu.VMEM((16, NC), F32),
            pltpu.SemaphoreType.DMA((N_MESSAGES,)),
            pltpu.SemaphoreType.DMA((N_MESSAGES,)),
            pltpu.SemaphoreType.DMA((N_LOCAL,)),
        ],
        compiler_params=pltpu.CompilerParams(
            collective_id=0, has_side_effects=True, vmem_limit_bytes=56 * 1024 * 1024
        ),
    )(queries, kv, w_out, gate_table, levels, span_mask, counts)


def solution(mesh):
    in_specs = (
        P(("rep", "span", "head"), None),
        P(("rep", "span", "head"), None, None),
        P("head", None),
        P(),
        P("rep"),
        P("rep", None),
        P("rep"),
    )
    out_specs = P(("rep", "span", "head"), None)
    return jax.shard_map(local, mesh=mesh, in_specs=in_specs, out_specs=out_specs, check_vma=False)
```

```python
import jax
import jax.numpy as jnp
from jax import lax
from jax.experimental import pallas as pl
from jax.experimental.pallas import tpu as pltpu
from jax.sharding import PartitionSpec as P

MESH = pl.DeviceIdType.MESH
HD = 128
SPAN = 1024
D = 6144
ROWS = 64
QT = 256
SHARD = 384
NC = 3072
QC = 768
EXP_SCALE = HD**-0.5 * 1.4426950408889634
F32 = jnp.float32
BF16 = jnp.bfloat16


class Names:
    def __init__(self):
        self.ids = {}

    def __call__(self, name):
        return self.ids.setdefault(name, len(self.ids))


N_MESSAGES = 130
N_LOCAL = 8


def kernel(
    q_hbm, kv_ref, w_hbm, gate_ref, levels_ref, mask_ref, counts_ref, out_ref,
    kv_st, q_buf, kv_buf, kp, ve, m_ref, acc, a_st, a_buf, w_buf, o_st, ra_l, ra_r, rb_l, rb_r,
    f_out, f_in, gate_row, send_sem, recv_sem, local_sem,
):
    span = lax.axis_index("span")
    head = lax.axis_index("head")
    y = lax.axis_index("rep")
    core = lax.rem(span, 2)
    zl = head // 4
    x = lax.rem(head, 4)
    z = (span // 2) * 4 + zl
    a = x // 2
    b = lax.rem(x, 2)

    def at_x(xx):
        return {"head": zl * 4 + xx}

    def at_z(zz):
        return {"span": (zz // 4) * 2 + core, "head": lax.rem(zz, 4) * 4 + x}

    def at_y(yy):
        return {"rep": yy}

    sibling = {"span": (span // 2) * 2 + 1 - core}
    x_peers = [lax.rem(x + d, 4) for d in range(4)]
    z_right, z_left = lax.rem(z + 1, 8), lax.rem(z + 7, 8)
    y_right, y_left = lax.rem(y + 1, 4), lax.rem(y + 3, 4)
    y_far = lax.rem(y + 2, 4)
    z_right2, z_left2 = lax.rem(z + 2, 8), lax.rem(z + 6, 8)
    parity = lax.rem(z, 2)
    z_pair = z + 1 - 2 * parity

    names = Names()
    sent = []

    def message(name, src, dst, where):
        number = names(name)
        return pltpu.make_async_remote_copy(
            src_ref=src, dst_ref=dst, send_sem=send_sem.at[number], recv_sem=recv_sem.at[number],
            device_id=where, device_id_type=MESH,
        )

    def send(name, src, dst, where):
        message(name, src(), dst(), where()).start()
        sent.append((name, src, dst, where))

    def drain(*kinds):
        for item in list(sent):
            if item[0].startswith(kinds):
                name, src, dst, where = item
                message(name, src(), dst(), where()).wait_send()
                sent.remove(item)

    def arrived(name, dst):
        message(name, dst, dst, sibling).wait_recv()

    barrier = pltpu.get_barrier_semaphore()
    peers = [at_x(x_peers[d]) for d in (1, 2, 3)]
    peers += [at_z(zz) for zz in (z_right, z_left, z_right2, z_left2)]
    peers += [at_y(yy) for yy in (y_right, y_left, y_far)]
    peers += [sibling]
    for peer in peers:
        pl.semaphore_signal(barrier, inc=1, device_id=peer, device_id_type=MESH)
    kv_st[0] = kv_ref[:, 0, :]
    kv_st[1] = kv_ref[:, 1, :]
    m_ref[...] = jnp.full(m_ref.shape, -1e30, F32)
    acc[...] = jnp.zeros(acc.shape, F32)
    pl.semaphore_wait(barrier, len(peers))

    def group_of(xx, g):
        return 4 * lax.rem(xx, 2) + 2 * g + xx // 2

    def cols(start, width):
        return pl.ds(pl.multiple_of(start, 128), width)

    def rows(start, width):
        return pl.ds(pl.multiple_of(start, 64), width)

    half = SHARD // 2
    WIDE = QC // 2

    def q_cols(n, of_core=None):
        return cols(n * QC + (core if of_core is None else of_core) * WIDE, WIDE)

    def w_own(start, size, side):
        return w_hbm.at[pl.ds(start, size), cols(side * NC + y * QC + core * WIDE, WIDE)]

    def w_at(start, size, n, of_core=None):
        return w_buf.at[pl.ds(start, size), q_cols(n, of_core)]

    def w_near():
        send("WR1", lambda: w_own(0, SHARD, 1 - parity), lambda: w_at(SHARD, SHARD, y), lambda: at_z(z_right))
        send("WL1", lambda: w_own(0, SHARD, 1 - parity), lambda: w_at(2 * SHARD, SHARD, y), lambda: at_z(z_left))

    def w_far():
        send("WR2", lambda: w_own(0, half, parity), lambda: w_at(3 * SHARD, half, y), lambda: at_z(z_right2))
        send("WL2", lambda: w_own(half, half, parity), lambda: w_at(3 * SHARD + half, half, y), lambda: at_z(z_left2))

    def y_out(slot):
        send("YR%d" % slot, lambda: w_at(slot * SHARD, SHARD, y), lambda: w_at(slot * SHARD, SHARD, y), lambda: at_y(y_right))
        send("YL%d" % slot, lambda: w_at(slot * SHARD, SHARD, y), lambda: w_at(slot * SHARD, SHARD, y), lambda: at_y(y_left))
        send("YF%d" % slot, lambda: w_at(slot * SHARD, SHARD, y), lambda: w_at(slot * SHARD, SHARD, y), lambda: at_y(y_far))

    def w_got_near():
        arrived("WR1", w_at(SHARD, SHARD, y))
        y_out(1)
        arrived("WL1", w_at(2 * SHARD, SHARD, y))
        y_out(2)

    def w_sibling(name, n):
        send("S" + name, lambda: w_at(SHARD, 3 * SHARD, n), lambda: w_at(SHARD, 3 * SHARD, n), lambda: sibling)

    def w_from_sibling(name, n):
        arrived("S" + name, w_at(SHARD, 3 * SHARD, n, 1 - core))

    def w_got_far():
        arrived("WR2", w_at(3 * SHARD, half, y))
        arrived("WL2", w_at(3 * SHARD + half, half, y))
        y_out(3)
        w_sibling("YO", y)

    def y_got(way, n):
        for slot in (1, 2, 3):
            arrived("%s%d" % (way, slot), w_at(slot * SHARD, SHARD, n))
        w_sibling(way, n)

    def kv_sibling(slot, g):
        send("KS%d%d" % (slot, g), lambda: kv_buf.at[slot, 0, g], lambda: kv_buf.at[slot, 1, g], lambda: sibling)

    def kv_from_sibling(slot, g):
        arrived("KS%d%d" % (slot, g), kv_buf.at[slot, 1, g])

    def kv_send(step, from_slot, g, right):
        to_slot = 2 * step - 1 if right else 2 * step
        if step == 4:
            to_slot = 7
        send(
            ("KR%d%d" if right else "KL%d%d") % (step, g),
            lambda: kv_buf.at[from_slot, 0, g],
            lambda: kv_buf.at[to_slot, 0, g],
            lambda: at_z(z_right if right else z_left),
        )

    def kv_step(step, g):
        from_left, from_right = 2 * step - 1, 2 * step
        arrived("KR%d%d" % (step, g), kv_buf.at[from_left, 0, g])
        if step < 3 or g == 0:
            kv_send(step + 1, from_left, g, True)
        arrived("KL%d%d" % (step, g), kv_buf.at[from_right, 0, g])
        if step < 3 or g == 1:
            kv_send(step + 1, from_right, g, False)
        kv_sibling(from_left, g)
        kv_sibling(from_right, g)

    def kv_last():
        arrived("KR40", kv_buf.at[7, 0, 0])
        kv_sibling(7, 0)
        arrived("KL41", kv_buf.at[7, 0, 1])
        kv_sibling(7, 1)

    def local_copy(number, src, dst):
        copy = pltpu.make_async_copy(src, dst, local_sem.at[number])
        copy.start()
        return copy

    def kv_across(d, g):
        send(
            "KX%d%d" % (d, g),
            lambda: kv_st.at[:, :, cols(group_of(x_peers[d], g) * HD, HD)],
            lambda: kv_buf.at[0, 0, g, :, rows(x * ROWS, ROWS), :],
            lambda: at_x(x_peers[d]),
        )

    def q_side(xx, turn):
        return lax.rem(1 - lax.rem(xx, 2) + turn, 2)

    def q_across(d, g, turn):
        start = lambda: group_of(x_peers[d], g) * 768 + q_side(x_peers[d], turn) * SHARD
        send(
            "QX%d%d%d" % (d, g, turn),
            lambda: q_hbm.at[:, cols(start(), SHARD)],
            lambda: q_buf.at[g, rows(x * ROWS, ROWS), cols(q_side(x_peers[d], turn) * SHARD, SHARD)],
            lambda: at_x(x_peers[d]),
        )

    def q_wait(g, turn):
        for d in (1, 3, 2):
            arrived(
                "QX%d%d%d" % (d, g, turn),
                q_buf.at[g, rows(x_peers[4 - d] * ROWS, ROWS), cols(q_side(x, turn) * SHARD, SHARD)],
            )

    for g in range(2):
        for d in (1, 3, 2):
            kv_across(d, g)
    kv_local = [
        local_copy(g, kv_st.at[:, :, cols(group_of(x, g) * HD, HD)], kv_buf.at[0, 0, g, :, rows(x * ROWS, ROWS), :])
        for g in range(2)
    ]
    w_near()
    for turn in range(2):
        for g in range(2):
            for d in (1, 3, 2):
                q_across(d, g, turn)
    q_local = [
        local_copy(2 + g, q_hbm.at[:, cols(group_of(x, g) * 768, 768)], q_buf.at[g, rows(x * ROWS, ROWS), :])
        for g in range(2)
    ]
    w_local = local_copy(4, w_hbm.at[:, cols(parity * NC, NC)], w_buf.at[pl.ds(0, SHARD), :])

    for g in range(2):
        kv_local[g].wait()
        for d in (1, 3, 2):
            arrived("KX%d%d" % (d, g), kv_buf.at[0, 0, g, :, rows(x_peers[4 - d] * ROWS, ROWS), :])
        kv_send(1, 0, g, True)
        kv_send(1, 0, g, False)
        kv_sibling(0, g)

    kv_step(1, 0)
    w_got_near()
    kv_step(1, 1)
    for copy in q_local:
        copy.wait()
    def prepare(tile, g):
        for slot in (2 * tile, 2 * tile + 1):
            kv_from_sibling(slot, g)
        for slot in (2 * tile, 2 * tile + 1):
            step = (slot + 1) // 2
            src_z = lax.rem(z + (8 - step if slot % 2 else step), 8)
            for rel in range(2):
                src_span = (src_z // 4) * 2 + (core if rel == 0 else 1 - core)
                limit = counts_ref[src_span] * mask_ref[span, src_span]
                place = lax.broadcasted_iota(jnp.int32, (QT, HD), 0) + lax.rem(src_z, 4) * QT
                keep = jnp.where(place < limit, 1.0, 0.0).astype(BF16)
                drop = jnp.where(place < limit, 0.0, 1.0).astype(BF16)
                at = pl.ds((slot - 2 * tile) * 512 + rel * 256, QT)
                stand_in = jnp.broadcast_to(kv_buf[0, 0, g, 0, 0:16, :].astype(F32)[0:1], (QT, HD)).astype(BF16)
                kp[g, at, :] = kv_buf[slot, rel, g, 0] * keep + stand_in * drop
                ve[g, at, 0:HD] = kv_buf[slot, rel, g, 1] * keep
                ve[g, at, HD : 2 * HD] = keep

    def a_place(place, shard, zz):
        d = lax.rem(shard - lax.rem(zz, 4) + 4, 4)
        slot = (lax.rem(d, 3) + 1) * jnp.minimum(d, 1)
        return a_buf.at[pl.ds(place * QT, QT), cols(slot * SHARD, SHARD)]

    partner = at_x(x + 1 - 2 * b)

    def a_across(g):
        send("AX%d" % g, lambda: a_st.at[g, 1 - b], lambda: a_place(0, 2 * b + g, z), lambda: partner)

    def a_own(g):
        local_copy(5 + g, a_st.at[g, b], a_place(0, 2 * b + g, z))
        send("AZ%d" % g, lambda: a_st.at[g, b], lambda: a_place(1, 2 * b + g, z_pair), lambda: at_z(z_pair))

    def a_forward(g):
        mine = lambda: a_place(0, 2 * (1 - b) + g, z)
        arrived("AX%d" % g, mine())
        send("AF%d" % g, mine, lambda: a_place(1, 2 * (1 - b) + g, z_pair), lambda: at_z(z_pair))

    def service(i):
        todo = {
            0: lambda: (q_wait(0, 0), prepare(0, 0)),
            1: lambda: (q_wait(1, 0), prepare(0, 1)),
            2: lambda: (kv_step(2, 0), q_wait(0, 1)),
            3: lambda: (kv_step(2, 1), q_wait(1, 1)),
            4: lambda: prepare(1, 0),
            5: lambda: prepare(1, 1),
            6: lambda: kv_step(3, 0),
            7: lambda: kv_step(3, 1),
            8: lambda: (prepare(2, 0), w_far()),
            9: lambda: prepare(2, 1),
            10: lambda: kv_last(),
            12: lambda: prepare(3, 0),
            13: lambda: prepare(3, 1),
            14: lambda: w_got_far(),
        }
        def quarter(t):
            for when, what in todo.items():
                if when // 4 == t:
                    pl.when(i == when)(lambda what=what: (what(), None)[1])

        for t in range(4):
            pl.when(i // 4 == t)(lambda t=t: quarter(t))

    def attend(i, carry):
        service(i)
        g = lax.rem(i, 2)
        side = lax.rem(1 - b + lax.rem(i // 2, 2), 2)
        heads = [side * 3 + j for j in range(3)]
        keys, values = kp[g], ve[g]
        queries = [q_buf[g, :, cols(h * HD, HD)] for h in heads]
        earlier = [m_ref[g, h] for h in heads]
        sums = [acc[g, h] for h in heads]
        latest, results = [], []

        def score(j):
            return lax.dot_general(queries[j], keys, (((1,), (1,)), ((), ())), preferred_element_type=F32)

        ahead = score(0)
        for j in range(3):
            scores = ahead
            if j < 2:
                ahead = score(j + 1)
            top = jnp.maximum(earlier[j], jnp.max(scores, axis=1, keepdims=True))
            latest.append(top)
            weights = jnp.exp2((scores - jnp.concatenate([top] * 8, axis=1)) * EXP_SCALE).astype(BF16)
            factor = jnp.exp2((earlier[j] - top) * EXP_SCALE)
            both = jnp.dot(weights, values, preferred_element_type=F32)
            results.append(sums[j] * jnp.concatenate([factor] * 2, axis=1) + both)
        for j in range(3):
            m_ref[g, heads[j]] = latest[j]
            acc[g, heads[j]] = results[j]

        @pl.when(i >= 12)
        def _():
            for j in range(3):
                h = side * 3 + j
                a_st[g, side, :, j * HD : (j + 1) * HD] = (acc[g, h, :, 0:HD] / acc[g, h, :, HD : 2 * HD]).astype(BF16)

            for when, what in {12: lambda: a_across(0), 13: lambda: a_across(1), 14: lambda: a_own(0), 15: lambda: a_own(1)}.items():
                pl.when(i == when)(what)

        return carry

    lax.fori_loop(0, 16, attend, 0)

    chosen = (lax.broadcasted_iota(jnp.int32, (16, 64), 1) == levels_ref[span]).astype(F32).astype(BF16)
    for part in range(2):
        gate_row[:, part * 1536 : (part + 1) * 1536] = jnp.dot(
            chosen, gate_ref[:, cols(parity * NC + part * 1536, 1536)], preferred_element_type=F32
        )

    drain("KX", "QX", "KR", "KL", "KS", "W")
    for g in range(2):
        a_forward(g)
    for g in range(2):
        pltpu.make_async_copy(a_st.at[g, b], a_place(0, 2 * b + g, z), local_sem.at[5 + g]).wait()
    w_local.wait()

    quarters = [y, y_left, y_right, y_far]
    x_right, x_left, x_far = x_peers[1], x_peers[3], x_peers[2]
    width = QC

    def project(k):
        tokens = pl.ds((k // 4) * QT, QT)
        start = quarters[k % 4] * QC

        def piece(n, carry):
            part = jnp.dot(a_buf[tokens, :], w_buf[:, cols(start + n * 256, 256)], preferred_element_type=F32)
            o_st[k, :, cols(n * 256, 256)] = part.astype(BF16)
            return carry

        lax.fori_loop(0, width // 256, piece, 0)
        h = width // 2
        send("RA%d" % k, lambda: o_st.at[k, rows(x_far * ROWS, ROWS), pl.ds(0, h)], lambda: ra_l.at[k, :, pl.ds(0, h)], lambda: at_x(x_right))
        send("LA%d" % k, lambda: o_st.at[k, rows(x_far * ROWS, ROWS), pl.ds(h, h)], lambda: ra_r.at[k, :, pl.ds(0, h)], lambda: at_x(x_left))

    def pass_on(k):
        h = width // 2
        arrived("RA%d" % k, ra_l.at[k, :, pl.ds(0, h)])
        mine = o_st[k, rows(x_right * ROWS, ROWS), 0:h].astype(F32)
        o_st[k, rows(x_right * ROWS, ROWS), 0:h] = (mine + ra_l[k, :, 0:h].astype(F32)).astype(BF16)
        send("RB%d" % k, lambda: o_st.at[k, rows(x_right * ROWS, ROWS), pl.ds(0, width)], lambda: rb_l.at[k, :, pl.ds(0, width)], lambda: at_x(x_right))
        arrived("LA%d" % k, ra_r.at[k, :, pl.ds(0, h)])
        mine = o_st[k, rows(x_left * ROWS, ROWS), h:width].astype(F32)
        o_st[k, rows(x_left * ROWS, ROWS), h:width] = (mine + ra_r[k, :, 0:h].astype(F32)).astype(BF16)
        send("LB%d" % k, lambda: o_st.at[k, rows(x_left * ROWS, ROWS), pl.ds(0, width)], lambda: rb_r.at[k, :, pl.ds(0, width)], lambda: at_x(x_left))

    def finish(k):
        arrived("RB%d" % k, rb_l.at[k, :, pl.ds(0, width)])
        arrived("LB%d" % k, rb_r.at[k, :, pl.ds(0, width)])
        total = o_st[k, rows(x * ROWS, ROWS), 0:width].astype(F32)
        total = total + rb_l[k, :, 0:width].astype(F32) + rb_r[k, :, 0:width].astype(F32)
        n = quarters[k % 4]
        owner = head if k < 4 else lax.rem(z_pair, 4) * 4 + x
        place = lax.broadcasted_iota(jnp.int32, (ROWS, width), 0) + owner * ROWS
        gated = total * gate_row[0:1, cols(n * QC, QC)]
        result = jnp.where(place < counts_ref[span], gated, 0.0).astype(BF16)
        if k < 4:
            out_ref[:, cols(parity * NC + n * QC, QC)] = result
        else:
            f_out[k - 4] = result
            send("F%d" % (k - 4), lambda: f_out.at[k - 4], lambda: f_in.at[k - 4], lambda: at_z(z_pair))

    def take(k):
        arrived("F%d" % k, f_in.at[k])
        out_ref[:, cols((1 - parity) * NC + quarters[k] * QC, QC)] = f_in[k]

    w_from_sibling("YO", y)
    project(0)
    y_got("YR", y_left)
    y_got("YL", y_right)
    w_from_sibling("YR", y_left)
    project(1)
    pass_on(0)
    w_from_sibling("YL", y_right)
    project(2)
    pass_on(1)
    pass_on(2)
    y_got("YF", y_far)
    for g in range(2):
        arrived("AZ%d" % g, a_place(1, 2 * b + g, z))
        arrived("AF%d" % g, a_place(1, 2 * (1 - b) + g, z))
    for k in (4, 5, 6):
        project(k)
    w_from_sibling("YF", y_far)
    project(7)
    pass_on(4)
    project(3)
    finish(0)
    pass_on(5)
    finish(1)
    pass_on(6)
    finish(2)
    pass_on(7)
    pass_on(3)
    drain("A", "Y", "S", "RA", "LA")
    for k in (4, 5, 6, 7):
        finish(k)
    for k in range(4):
        take(k)
    finish(3)
    drain("")


def local(queries, key_value, w_out, gate_table, levels, span_mask, counts):
    anywhere = pl.BlockSpec(memory_space=pl.ANY)
    vmem = pl.BlockSpec(memory_space=pltpu.VMEM)
    smem = pl.BlockSpec(memory_space=pltpu.SMEM)
    return pl.pallas_call(
        kernel,
        out_shape=jax.ShapeDtypeStruct((ROWS, D), BF16),
        in_specs=[anywhere, vmem, anywhere, vmem, smem, smem, smem],
        out_specs=vmem,
        scratch_shapes=[
            pltpu.VMEM((2, ROWS, 1024), BF16),
            pltpu.VMEM((2, QT, 768), BF16),
            pltpu.VMEM((8, 2, 2, 2, QT, HD), BF16),
            pltpu.VMEM((2, 1024, HD), BF16),
            pltpu.VMEM((2, 1024, 2 * HD), BF16),
            pltpu.VMEM((2, 6, QT, HD), F32),
            pltpu.VMEM((2, 6, QT, 2 * HD), F32),
            pltpu.VMEM((2, 2, QT, SHARD), BF16),
            pltpu.VMEM((2 * QT, 4 * SHARD), BF16),
            pltpu.VMEM((4 * SHARD, NC), BF16),
            pltpu.VMEM((8, QT, QC), BF16),
            pltpu.VMEM((8, ROWS, QC // 2), BF16),
            pltpu.VMEM((8, ROWS, QC // 2), BF16),
            pltpu.VMEM((8, ROWS, QC), BF16),
            pltpu.VMEM((8, ROWS, QC), BF16),
            pltpu.VMEM((4, ROWS, QC), BF16),
            pltpu.VMEM((4, ROWS, QC), BF16),
            pltpu.VMEM((16, NC), F32),
            pltpu.SemaphoreType.DMA((N_MESSAGES,)),
            pltpu.SemaphoreType.DMA((N_MESSAGES,)),
            pltpu.SemaphoreType.DMA((N_LOCAL,)),
        ],
        compiler_params=pltpu.CompilerParams(
            collective_id=0, has_side_effects=True, vmem_limit_bytes=56 * 1024 * 1024
        ),
    )(queries, key_value, w_out, gate_table, levels, span_mask, counts)


def solution(mesh):
    in_specs = (
        P(("rep", "span", "head"), None),
        P(("rep", "span", "head"), None, None),
        P("head", None),
        P(),
        P("rep"),
        P("rep", None),
        P("rep"),
    )
    out_specs = P(("rep", "span", "head"), None)
    return jax.shard_map(local, mesh=mesh, in_specs=in_specs, out_specs=out_specs, check_vma=False)
```

```python
import jax
import jax.numpy as jnp
from jax import lax
from jax.experimental import pallas as pl
from jax.experimental.pallas import tpu as pltpu
from jax.sharding import PartitionSpec as P

MESH = pl.DeviceIdType.MESH
HD = 128
SPAN = 1024
D = 6144
ROWS = 64
QT = 256
SHARD = 384
NC = 3072
QC = 768
EXP_SCALE = HD**-0.5 * 1.4426950408889634
F32 = jnp.float32
BF16 = jnp.bfloat16


class Names:
    def __init__(self):
        self.ids = {}

    def __call__(self, name):
        return self.ids.setdefault(name, len(self.ids))


N_MESSAGES = 130
N_LOCAL = 8


def kernel(
    q_hbm, kv_ref, w_hbm, gate_hbm, levels_ref, mask_ref, counts_ref, out_ref,
    gate_buf, kv_st, q_buf, kv_buf, kp, ve, m_ref, acc, a_st, a_buf, w_buf, o_st, ra_l, ra_r, rb_l, rb_r,
    f_out, f_in, gate_row, send_sem, recv_sem, local_sem,
):
    span = lax.axis_index("span")
    head = lax.axis_index("head")
    y = lax.axis_index("rep")
    core = lax.rem(span, 2)
    zl = head // 4
    x = lax.rem(head, 4)
    z = (span // 2) * 4 + zl
    a = x // 2
    b = lax.rem(x, 2)

    def at_x(xx):
        return {"head": zl * 4 + xx}

    def at_z(zz):
        return {"span": (zz // 4) * 2 + core, "head": lax.rem(zz, 4) * 4 + x}

    def at_y(yy):
        return {"rep": yy}

    sibling = {"span": (span // 2) * 2 + 1 - core}
    x_peers = [lax.rem(x + d, 4) for d in range(4)]
    z_right, z_left = lax.rem(z + 1, 8), lax.rem(z + 7, 8)
    y_right, y_left = lax.rem(y + 1, 4), lax.rem(y + 3, 4)
    y_far = lax.rem(y + 2, 4)
    z_right2, z_left2 = lax.rem(z + 2, 8), lax.rem(z + 6, 8)
    parity = lax.rem(z, 2)
    z_pair = z + 1 - 2 * parity

    names = Names()
    sent = []

    def message(name, src, dst, where):
        number = names(name)
        return pltpu.make_async_remote_copy(
            src_ref=src, dst_ref=dst, send_sem=send_sem.at[number], recv_sem=recv_sem.at[number],
            device_id=where, device_id_type=MESH,
        )

    def send(name, src, dst, where):
        message(name, src(), dst(), where()).start()
        sent.append((name, src, dst, where))

    def drain(*kinds):
        for item in list(sent):
            if item[0].startswith(kinds):
                name, src, dst, where = item
                message(name, src(), dst(), where()).wait_send()
                sent.remove(item)

    def arrived(name, dst):
        message(name, dst, dst, sibling).wait_recv()

    barrier = pltpu.get_barrier_semaphore()
    peers = [at_x(x_peers[d]) for d in (1, 2, 3)]
    peers += [at_z(zz) for zz in (z_right, z_left, z_right2, z_left2)]
    peers += [at_y(yy) for yy in (y_right, y_left, y_far)]
    peers += [sibling]
    for peer in peers:
        pl.semaphore_signal(barrier, inc=1, device_id=peer, device_id_type=MESH)
    kv_st[0] = kv_ref[:, 0, :]
    kv_st[1] = kv_ref[:, 1, :]
    pl.semaphore_wait(barrier, len(peers))

    def group_of(xx, g):
        return 4 * lax.rem(xx, 2) + 2 * g + xx // 2

    def cols(start, width):
        return pl.ds(pl.multiple_of(start, 128), width)

    def rows(start, width):
        return pl.ds(pl.multiple_of(start, 64), width)

    half = SHARD // 2
    WIDE = QC // 2

    def q_cols(n, of_core=None):
        return cols(n * QC + (core if of_core is None else of_core) * WIDE, WIDE)

    def w_own(start, size, side):
        return w_hbm.at[pl.ds(start, size), cols(side * NC + y * QC + core * WIDE, WIDE)]

    def w_at(start, size, n, of_core=None):
        return w_buf.at[pl.ds(start, size), q_cols(n, of_core)]

    def w_near():
        send("WR1", lambda: w_own(0, SHARD, 1 - parity), lambda: w_at(SHARD, SHARD, y), lambda: at_z(z_right))
        send("WL1", lambda: w_own(0, SHARD, 1 - parity), lambda: w_at(2 * SHARD, SHARD, y), lambda: at_z(z_left))

    def w_far():
        send("WR2", lambda: w_own(0, half, parity), lambda: w_at(3 * SHARD, half, y), lambda: at_z(z_right2))
        send("WL2", lambda: w_own(half, half, parity), lambda: w_at(3 * SHARD + half, half, y), lambda: at_z(z_left2))

    def y_out(slot):
        send("YR%d" % slot, lambda: w_at(slot * SHARD, SHARD, y), lambda: w_at(slot * SHARD, SHARD, y), lambda: at_y(y_right))
        send("YL%d" % slot, lambda: w_at(slot * SHARD, SHARD, y), lambda: w_at(slot * SHARD, SHARD, y), lambda: at_y(y_left))
        send("YF%d" % slot, lambda: w_at(slot * SHARD, SHARD, y), lambda: w_at(slot * SHARD, SHARD, y), lambda: at_y(y_far))

    def w_got_near():
        arrived("WR1", w_at(SHARD, SHARD, y))
        y_out(1)
        arrived("WL1", w_at(2 * SHARD, SHARD, y))
        y_out(2)

    PARTS = {"A": (SHARD, 2 * SHARD), "B": (3 * SHARD, SHARD)}

    def w_sibling(name, n, part):
        start, size = PARTS[part]
        send("S" + name + part, lambda: w_at(start, size, n), lambda: w_at(start, size, n), lambda: sibling)

    def w_from_sibling(name, n):
        for part in PARTS:
            start, size = PARTS[part]
            arrived("S" + name + part, w_at(start, size, n, 1 - core))

    def w_got_far():
        arrived("WR2", w_at(3 * SHARD, half, y))
        arrived("WL2", w_at(3 * SHARD + half, half, y))
        y_out(3)
        w_sibling("YO", y, "B")

    def y_got(way, n, part):
        for slot in (1, 2) if part == "A" else (3,):
            arrived("%s%d" % (way, slot), w_at(slot * SHARD, SHARD, n))
        w_sibling(way, n, part)

    def kv_sibling(slot, g):
        send("KS%d%d" % (slot, g), lambda: kv_buf.at[slot, 0, g], lambda: kv_buf.at[slot, 1, g], lambda: sibling)

    def kv_from_sibling(slot, g):
        arrived("KS%d%d" % (slot, g), kv_buf.at[slot, 1, g])

    def kv_send(step, from_slot, g, right):
        to_slot = 2 * step - 1 if right else 2 * step
        if step == 4:
            to_slot = 7
        send(
            ("KR%d%d" if right else "KL%d%d") % (step, g),
            lambda: kv_buf.at[from_slot, 0, g],
            lambda: kv_buf.at[to_slot, 0, g],
            lambda: at_z(z_right if right else z_left),
        )

    def kv_step(step, g):
        from_left, from_right = 2 * step - 1, 2 * step
        arrived("KR%d%d" % (step, g), kv_buf.at[from_left, 0, g])
        if step < 3 or g == 0:
            kv_send(step + 1, from_left, g, True)
        arrived("KL%d%d" % (step, g), kv_buf.at[from_right, 0, g])
        if step < 3 or g == 1:
            kv_send(step + 1, from_right, g, False)
        kv_sibling(from_left, g)
        kv_sibling(from_right, g)

    def kv_last():
        arrived("KR40", kv_buf.at[7, 0, 0])
        kv_sibling(7, 0)
        arrived("KL41", kv_buf.at[7, 0, 1])
        kv_sibling(7, 1)

    def local_copy(number, src, dst):
        copy = pltpu.make_async_copy(src, dst, local_sem.at[number])
        copy.start()
        return copy

    def kv_across(d, g):
        send(
            "KX%d%d" % (d, g),
            lambda: kv_st.at[:, :, cols(group_of(x_peers[d], g) * HD, HD)],
            lambda: kv_buf.at[0, 0, g, :, rows(x * ROWS, ROWS), :],
            lambda: at_x(x_peers[d]),
        )

    def q_side(xx, turn):
        return lax.rem(1 - lax.rem(xx, 2) + turn, 2)

    def q_across(d, g, turn):
        start = lambda: group_of(x_peers[d], g) * 768 + q_side(x_peers[d], turn) * SHARD
        send(
            "QX%d%d%d" % (d, g, turn),
            lambda: q_hbm.at[:, cols(start(), SHARD)],
            lambda: q_buf.at[g, rows(x * ROWS, ROWS), cols(q_side(x_peers[d], turn) * SHARD, SHARD)],
            lambda: at_x(x_peers[d]),
        )

    def q_wait(g, turn):
        for d in (1, 3, 2):
            arrived(
                "QX%d%d%d" % (d, g, turn),
                q_buf.at[g, rows(x_peers[4 - d] * ROWS, ROWS), cols(q_side(x, turn) * SHARD, SHARD)],
            )

    for g in range(2):
        for d in (1, 3, 2):
            kv_across(d, g)
    kv_local = [
        local_copy(g, kv_st.at[:, :, cols(group_of(x, g) * HD, HD)], kv_buf.at[0, 0, g, :, rows(x * ROWS, ROWS), :])
        for g in range(2)
    ]
    w_near()
    for turn in range(2):
        for g in range(2):
            for d in (1, 3, 2):
                q_across(d, g, turn)
    q_local = [
        local_copy(2 + g, q_hbm.at[:, cols(group_of(x, g) * 768, 768)], q_buf.at[g, rows(x * ROWS, ROWS), :])
        for g in range(2)
    ]
    gate_local = local_copy(7, gate_hbm.at[:, cols(parity * NC, NC)], gate_buf)
    w_local = local_copy(4, w_hbm.at[:, cols(parity * NC, NC)], w_buf.at[pl.ds(0, SHARD), :])

    m_ref[...] = jnp.full(m_ref.shape, -1e30, F32)
    acc[...] = jnp.zeros(acc.shape, F32)

    for g in range(2):
        kv_local[g].wait()
        for d in (1, 3, 2):
            arrived("KX%d%d" % (d, g), kv_buf.at[0, 0, g, :, rows(x_peers[4 - d] * ROWS, ROWS), :])
        kv_send(1, 0, g, True)
        kv_send(1, 0, g, False)
        kv_sibling(0, g)

    kv_step(1, 0)
    w_got_near()
    kv_step(1, 1)
    for copy in q_local:
        copy.wait()
    def prepare(tile, g):
        for slot in (2 * tile, 2 * tile + 1):
            kv_from_sibling(slot, g)
        for slot in (2 * tile, 2 * tile + 1):
            step = (slot + 1) // 2
            src_z = lax.rem(z + (8 - step if slot % 2 else step), 8)
            for rel in range(2):
                src_span = (src_z // 4) * 2 + (core if rel == 0 else 1 - core)
                limit = counts_ref[src_span] * mask_ref[span, src_span]
                place = lax.broadcasted_iota(jnp.int32, (QT, HD), 0) + lax.rem(src_z, 4) * QT
                keep = jnp.where(place < limit, 1.0, 0.0).astype(BF16)
                drop = jnp.where(place < limit, 0.0, 1.0).astype(BF16)
                at = pl.ds((slot - 2 * tile) * 512 + rel * 256, QT)
                stand_in = jnp.broadcast_to(kv_buf[0, 0, g, 0, 0:16, :].astype(F32)[0:1], (QT, HD)).astype(BF16)
                kp[g, at, :] = kv_buf[slot, rel, g, 0] * keep + stand_in * drop
                ve[g, at, 0:HD] = kv_buf[slot, rel, g, 1] * keep
                ve[g, at, HD : 2 * HD] = keep

    def a_place(place, shard, zz):
        d = lax.rem(shard - lax.rem(zz, 4) + 4, 4)
        slot = (lax.rem(d, 3) + 1) * jnp.minimum(d, 1)
        return a_buf.at[pl.ds(place * QT, QT), cols(slot * SHARD, SHARD)]

    partner = at_x(x + 1 - 2 * b)

    def a_across(g):
        send("AX%d" % g, lambda: a_st.at[g, 1 - b], lambda: a_place(0, 2 * b + g, z), lambda: partner)

    def a_own(g):
        local_copy(5 + g, a_st.at[g, b], a_place(0, 2 * b + g, z))
        send("AZ%d" % g, lambda: a_st.at[g, b], lambda: a_place(1, 2 * b + g, z_pair), lambda: at_z(z_pair))

    def a_forward(g):
        mine = lambda: a_place(0, 2 * (1 - b) + g, z)
        arrived("AX%d" % g, mine())
        send("AF%d" % g, mine, lambda: a_place(1, 2 * (1 - b) + g, z_pair), lambda: at_z(z_pair))

    def service(i):
        todo = {
            0: lambda: (q_wait(0, 0), prepare(0, 0)),
            1: lambda: (q_wait(1, 0), prepare(0, 1)),
            2: lambda: (kv_step(2, 0), q_wait(0, 1)),
            3: lambda: (kv_step(2, 1), q_wait(1, 1)),
            4: lambda: prepare(1, 0),
            5: lambda: prepare(1, 1),
            6: lambda: (kv_step(3, 0), w_sibling("YO", y, "A")),
            7: lambda: kv_step(3, 1),
            8: lambda: (prepare(2, 0), w_far()),
            9: lambda: prepare(2, 1),
            10: lambda: kv_last(),
            12: lambda: prepare(3, 0),
            13: lambda: prepare(3, 1),
            14: lambda: w_got_far(),
        }
        def quarter(t):
            for when, what in todo.items():
                if when // 4 == t:
                    pl.when(i == when)(lambda what=what: (what(), None)[1])

        for t in range(4):
            pl.when(i // 4 == t)(lambda t=t: quarter(t))

    def attend(i, carry):
        service(i)
        g = lax.rem(i, 2)
        side = lax.rem(1 - b + lax.rem(i // 2, 2), 2)
        heads = [side * 3 + j for j in range(3)]
        keys, values = kp[g], ve[g]
        queries = [q_buf[g, :, cols(h * HD, HD)] for h in heads]
        earlier = [m_ref[g, h] for h in heads]
        sums = [acc[g, h] for h in heads]
        latest, results = [], []

        def score(j):
            return lax.dot_general(queries[j], keys, (((1,), (1,)), ((), ())), preferred_element_type=F32)

        ahead = score(0)
        for j in range(3):
            scores = ahead
            if j < 2:
                ahead = score(j + 1)
            top = jnp.maximum(earlier[j], jnp.max(scores, axis=1, keepdims=True))
            latest.append(top)
            weights = jnp.exp2((scores - jnp.concatenate([top] * 8, axis=1)) * EXP_SCALE).astype(BF16)
            factor = jnp.exp2((earlier[j] - top) * EXP_SCALE)
            both = jnp.dot(weights, values, preferred_element_type=F32)
            results.append(sums[j] * jnp.concatenate([factor] * 2, axis=1) + both)
        for j in range(3):
            m_ref[g, heads[j]] = latest[j]
            acc[g, heads[j]] = results[j]

        @pl.when(i >= 12)
        def _():
            for j in range(3):
                h = side * 3 + j
                a_st[g, side, :, j * HD : (j + 1) * HD] = (acc[g, h, :, 0:HD] / acc[g, h, :, HD : 2 * HD]).astype(BF16)

            for when, what in {12: lambda: a_across(0), 13: lambda: a_across(1), 14: lambda: a_own(0), 15: lambda: a_own(1)}.items():
                pl.when(i == when)(what)

        return carry

    lax.fori_loop(0, 16, attend, 0)

    chosen = (lax.broadcasted_iota(jnp.int32, (16, 64), 1) == levels_ref[span]).astype(F32).astype(BF16)
    gate_local.wait()
    for part in range(2):
        gate_row[:, part * 1536 : (part + 1) * 1536] = jnp.dot(
            chosen, gate_buf[:, part * 1536 : (part + 1) * 1536], preferred_element_type=F32
        )

    drain("KX", "QX", "KR", "KL", "KS", "W")
    y_got("YR", y_left, "A")
    y_got("YL", y_right, "A")
    for g in range(2):
        a_forward(g)
    for g in range(2):
        pltpu.make_async_copy(a_st.at[g, b], a_place(0, 2 * b + g, z), local_sem.at[5 + g]).wait()
    w_local.wait()

    quarters = [y, y_left, y_right, y_far]
    x_right, x_left, x_far = x_peers[1], x_peers[3], x_peers[2]
    width = QC

    def project(k):
        tokens = pl.ds((k // 4) * QT, QT)
        start = quarters[k % 4] * QC

        def piece(n, carry):
            part = jnp.dot(a_buf[tokens, :], w_buf[:, cols(start + n * 256, 256)], preferred_element_type=F32)
            o_st[k, :, cols(n * 256, 256)] = part.astype(BF16)
            return carry

        lax.fori_loop(0, width // 256, piece, 0)
        h = width // 2
        send("RA%d" % k, lambda: o_st.at[k, rows(x_far * ROWS, ROWS), pl.ds(0, h)], lambda: ra_l.at[k, :, pl.ds(0, h)], lambda: at_x(x_right))
        send("LA%d" % k, lambda: o_st.at[k, rows(x_far * ROWS, ROWS), pl.ds(h, h)], lambda: ra_r.at[k, :, pl.ds(0, h)], lambda: at_x(x_left))

    def pass_on(k):
        h = width // 2
        arrived("RA%d" % k, ra_l.at[k, :, pl.ds(0, h)])
        mine = o_st[k, rows(x_right * ROWS, ROWS), 0:h].astype(F32)
        o_st[k, rows(x_right * ROWS, ROWS), 0:h] = (mine + ra_l[k, :, 0:h].astype(F32)).astype(BF16)
        send("RB%d" % k, lambda: o_st.at[k, rows(x_right * ROWS, ROWS), pl.ds(0, width)], lambda: rb_l.at[k, :, pl.ds(0, width)], lambda: at_x(x_right))
        arrived("LA%d" % k, ra_r.at[k, :, pl.ds(0, h)])
        mine = o_st[k, rows(x_left * ROWS, ROWS), h:width].astype(F32)
        o_st[k, rows(x_left * ROWS, ROWS), h:width] = (mine + ra_r[k, :, 0:h].astype(F32)).astype(BF16)
        send("LB%d" % k, lambda: o_st.at[k, rows(x_left * ROWS, ROWS), pl.ds(0, width)], lambda: rb_r.at[k, :, pl.ds(0, width)], lambda: at_x(x_left))

    def finish(k):
        arrived("RB%d" % k, rb_l.at[k, :, pl.ds(0, width)])
        arrived("LB%d" % k, rb_r.at[k, :, pl.ds(0, width)])
        total = o_st[k, rows(x * ROWS, ROWS), 0:width].astype(F32)
        total = total + rb_l[k, :, 0:width].astype(F32) + rb_r[k, :, 0:width].astype(F32)
        n = quarters[k % 4]
        owner = head if k < 4 else lax.rem(z_pair, 4) * 4 + x
        place = lax.broadcasted_iota(jnp.int32, (ROWS, width), 0) + owner * ROWS
        gated = total * gate_row[0:1, cols(n * QC, QC)]
        result = jnp.where(place < counts_ref[span], gated, 0.0).astype(BF16)
        if k < 4:
            out_ref[:, cols(parity * NC + n * QC, QC)] = result
        else:
            f_out[k - 4] = result
            send("F%d" % (k - 4), lambda: f_out.at[k - 4], lambda: f_in.at[k - 4], lambda: at_z(z_pair))

    def take(k):
        arrived("F%d" % k, f_in.at[k])
        out_ref[:, cols((1 - parity) * NC + quarters[k] * QC, QC)] = f_in[k]

    w_from_sibling("YO", y)
    project(0)
    y_got("YR", y_left, "B")
    y_got("YL", y_right, "B")
    y_got("YF", y_far, "A")
    w_from_sibling("YR", y_left)
    project(1)
    pass_on(0)
    w_from_sibling("YL", y_right)
    project(2)
    pass_on(1)
    pass_on(2)
    y_got("YF", y_far, "B")
    for g in range(2):
        arrived("AZ%d" % g, a_place(1, 2 * b + g, z))
        arrived("AF%d" % g, a_place(1, 2 * (1 - b) + g, z))
    for k in (4, 5, 6):
        project(k)
    w_from_sibling("YF", y_far)
    project(7)
    pass_on(4)
    project(3)
    finish(0)
    pass_on(5)
    finish(1)
    pass_on(6)
    finish(2)
    pass_on(7)
    pass_on(3)
    drain("A", "Y", "S", "RA", "LA")
    for k in (4, 5, 6, 7):
        finish(k)
    for k in range(4):
        take(k)
    finish(3)
    drain("")


def local(queries, key_value, w_out, gate_table, levels, span_mask, counts):
    anywhere = pl.BlockSpec(memory_space=pl.ANY)
    vmem = pl.BlockSpec(memory_space=pltpu.VMEM)
    smem = pl.BlockSpec(memory_space=pltpu.SMEM)
    return pl.pallas_call(
        kernel,
        out_shape=jax.ShapeDtypeStruct((ROWS, D), BF16),
        in_specs=[anywhere, vmem, anywhere, anywhere, smem, smem, smem],
        out_specs=vmem,
        scratch_shapes=[
            pltpu.VMEM((64, NC), BF16),
            pltpu.VMEM((2, ROWS, 1024), BF16),
            pltpu.VMEM((2, QT, 768), BF16),
            pltpu.VMEM((8, 2, 2, 2, QT, HD), BF16),
            pltpu.VMEM((2, 1024, HD), BF16),
            pltpu.VMEM((2, 1024, 2 * HD), BF16),
            pltpu.VMEM((2, 6, QT, HD), F32),
            pltpu.VMEM((2, 6, QT, 2 * HD), F32),
            pltpu.VMEM((2, 2, QT, SHARD), BF16),
            pltpu.VMEM((2 * QT, 4 * SHARD), BF16),
            pltpu.VMEM((4 * SHARD, NC), BF16),
            pltpu.VMEM((8, QT, QC), BF16),
            pltpu.VMEM((8, ROWS, QC // 2), BF16),
            pltpu.VMEM((8, ROWS, QC // 2), BF16),
            pltpu.VMEM((8, ROWS, QC), BF16),
            pltpu.VMEM((8, ROWS, QC), BF16),
            pltpu.VMEM((4, ROWS, QC), BF16),
            pltpu.VMEM((4, ROWS, QC), BF16),
            pltpu.VMEM((16, NC), F32),
            pltpu.SemaphoreType.DMA((N_MESSAGES,)),
            pltpu.SemaphoreType.DMA((N_MESSAGES,)),
            pltpu.SemaphoreType.DMA((N_LOCAL,)),
        ],
        compiler_params=pltpu.CompilerParams(
            collective_id=0, has_side_effects=True, vmem_limit_bytes=56 * 1024 * 1024
        ),
    )(queries, key_value, w_out, gate_table, levels, span_mask, counts)


def solution(mesh):
    in_specs = (
        P(("rep", "span", "head"), None),
        P(("rep", "span", "head"), None, None),
        P("head", None),
        P(),
        P("rep"),
        P("rep", None),
        P("rep"),
    )
    out_specs = P(("rep", "span", "head"), None)
    return jax.shard_map(local, mesh=mesh, in_specs=in_specs, out_specs=out_specs, check_vma=False)
```
